32 devices in a mesh: ctx: 4 (over y, x), head: 8 (over z, core).
Axes of the slice: x: 2, y: 2, z: 4, core: 2. Of those that a mesh axis runs over, the one named last changes fastest.
Arguments:
- queries: bfloat16 [4096, 4096], P('ctx', 'head'), may hold values from -6 to 6
- key_heads: bfloat16 [4096, 4096], P('ctx', 'head'), may hold values from -8 to 8
- value_heads: bfloat16 [4096, 4096], P('ctx', 'head'), may hold values from -120 to 120
- out_gain: bfloat16 [4096], P('head'), may hold values from 0.099609375 to 1.8984375
- out_weight: bfloat16 [4096, 2048], P('head'), may hold values from -0.09375 to 0.09375
- residual: bfloat16 [4096, 2048], P(('ctx', 'head')), may hold values from -36 to 36
- norm_gain: bfloat16 [2048], replicated, may hold values from 0.099609375 to 1.8984375
- routes: int32 [4096, 8], P(('ctx', 'head')), may hold values from 0 to 127, all different within a row; in each aligned block of 128 rows (0 to 127, 128 to 255, ...) at most 10 rows name the same one
- route_weights: float32 [4096, 8], P(('ctx', 'head')), may hold values from 0.02 to 0.4
- cotangent: bfloat16 [4096, 2048], P(('ctx', 'head')), may hold values from -6 to 6
- w_gate: bfloat16 [128, 2048, 768], P(('ctx', 'head')), may hold values from -0.125 to 0.125
- w_up: bfloat16 [128, 2048, 768], P(('ctx', 'head')), may hold values from -0.125 to 0.125
- w_down: bfloat16 [128, 768, 2048], P(('ctx', 'head')), may hold values from -0.21875 to 0.21875
Outputs:
- hidden_out: bfloat16 [4096, 2048], P(('ctx', 'head'))
- grad_gate: bfloat16 [128, 2048, 768], P(('ctx', 'head'))
- grad_up: bfloat16 [128, 2048, 768], P(('ctx', 'head'))
- grad_down: bfloat16 [128, 768, 2048], P(('ctx', 'head'))
The draws below stay inside these ranges and needn't reach their ends.
Inputs may be any that keep to these rules, and one draw needn't show every extreme that they name: `routes`: each row names 8 different experts. Within each aligned block of 128 rows no expert is named by more than 10 rows; in some blocks an expert is named by exactly 10 rows.
All inputs are finite; a program needn't handle non-finite values.
Results may differ from the reference program's by a relative error of at most 0.025.
Values may be sent and summed in bfloat16 or wider, within the bound.
A program may use at most 192 MiB of HBM per device.

```python
import math
import jax
import jax.numpy as jnp
import numpy as np
from jax import lax

D = 2048
FF = 768
HEADS = 32
HD = 128
EXPERTS = 128
TOPK = 8
TOK_DEV = 128
CAP = 10
TOKENS = 4096
N_CTX = 4
N_HEAD = 8


def draw_key_heads(key, part):
    entry_key, jitter_key, slope_key, base_key = jax.random.split(key, 4)
    fraction = jnp.arange(TOKENS).astype(jnp.float32) / TOKENS - 0.5
    jitter = jax.random.uniform(jitter_key, (TOKENS, 1), jnp.float32, -0.75, 0.75)
    slope = jax.random.uniform(slope_key, (HEADS,), jnp.float32, -5.0, 5.0)
    base = jax.random.uniform(base_key, (HEADS,), jnp.float32, -1.0, 0.5)
    offset_heads = base[None, :] + slope[None, :] * fraction[:, None]
    offset = jnp.repeat(offset_heads, HD, axis=1)
    entries = jnp.clip(jax.random.normal(entry_key, (TOKENS, HEADS * HD), jnp.float32), -4.0, 4.0)
    return jnp.clip(entries + offset + jitter, -8.0, 8.0).astype(jnp.bfloat16)


def draw_value_heads(key, part):
    columns = jnp.arange(HEADS * HD) // HD
    position = columns.astype(jnp.float32) / (HEADS - 1)
    entries = jnp.clip(jax.random.normal(key, (TOKENS, HEADS * HD), jnp.float32), -4.0, 4.0)
    column_scale = 10.0 ** position
    return (entries * column_scale[None, :]).astype(jnp.bfloat16)


def draw_residual(key, part):
    row_key, column_key, entry_key = jax.random.split(key, 3)
    row_scale = jnp.exp(jax.random.uniform(row_key, (TOKENS, 1), jnp.float32, math.log(0.3), math.log(3.0)))
    column_scale = jnp.exp(jax.random.uniform(column_key, (1, D), jnp.float32, math.log(0.3), math.log(3.0)))
    entries = jnp.clip(jax.random.normal(entry_key, (TOKENS, D), jnp.float32), -4.0, 4.0)
    return jnp.clip(entries * row_scale * column_scale, -36.0, 36.0).astype(jnp.bfloat16)


def level_of(key, dims, cuts, smallest, top_value):
    def one(dim, parts):
        heights = jax.random.uniform(jax.random.fold_in(jax.random.fold_in(key, 6), dim), (parts,), jnp.float32, smallest / len(cuts), top_value / len(cuts))
        return jnp.repeat(jnp.exp(heights), dims[dim] // parts).reshape((-1,) + (1,) * (len(dims) - dim - 1))

    loudness = one(*cuts[0])
    for cut in cuts[1:]:
        loudness = loudness * one(*cut)
    return loudness


def assign_block(rng, own, number, rows, count, top, most, skew):
    order = jax.random.permutation(rng, count)
    heavy_load, usual = load_shares(count, rows * top, most, skew, True), load_shares(count, rows * top, most, skew, False)
    places = jnp.arange(count)

    def named(lengths, rotation):
        used = int((lengths > 0).sum())
        fixed = max(1, used // 4)
        passed = fixed + (places - fixed + rotation * (used - fixed)) % max(1, count - fixed)
        return jnp.zeros((count,), jnp.int32).at[order[jnp.where(places < fixed, places, passed)]].set(jnp.asarray(lengths, jnp.int32))

    lengths = jnp.where(number % 4 == 0, named(heavy_load, number // 4), named(usual, number - number // 4 - 1))
    mixed = jax.random.permutation(jax.random.fold_in(own, 3), count)
    giver, sink = mixed[0:count // 2 * 2:2], mixed[1:count // 2 * 2:2]
    slack = jnp.minimum(lengths[giver] - 1, most - lengths[sink]) // 2
    slack = jnp.where((giver == order[0]) | (sink == order[0]) | (lengths[sink] == 0), 0, jnp.maximum(slack, 0))
    passed = jax.random.randint(jax.random.fold_in(own, 4), (count // 2,), 0, 1 << 20) % (slack + 1)
    lengths = lengths.at[giver].add(-passed).at[sink].add(passed)
    items = jnp.searchsorted(jnp.cumsum(lengths), jnp.arange(rows * top), side="right").astype(jnp.int32)
    grid = items.reshape(top, rows).T
    grid = grid[jax.random.permutation(jax.random.fold_in(own, 1), rows)]
    rotation = jax.random.randint(jax.random.fold_in(own, 2), (rows, 1), 0, top)
    return jnp.take_along_axis(grid, (jnp.arange(top)[None, :] + rotation) % top, axis=1)


def load_shares(number_of, total, most, lean, full):
    portions = [(1 << 20) // math.isqrt(grade ** lean) + 1 for grade in range(1, number_of + 1)]
    largest = most if full else min(most, max(-(-total // number_of), total * portions[0] // sum(portions)))
    least = 1 if total - largest >= number_of - 1 else 0
    counts, rest = [largest] + [least] * (number_of - 1), total - largest - least * (number_of - 1)
    while rest > 0:
        free = [i for i in range(1, number_of) if counts[i] < largest] or [i for i in range(1, number_of) if counts[i] < most]
        whole, remaining = sum([portions[i] for i in free]), rest
        for i in free:
            more = min(most - counts[i], max(1, remaining * portions[i] // whole), rest)
            counts[i] = counts[i] + more
            rest = rest - more
    return np.array(counts)


def scatter_about(stream_key, dims, scale, bound, shards=(), held_as=jnp.bfloat16):
    values = scale * jax.random.normal(stream_key, dims, jnp.float32)
    if shards:
        values = values * level_of(stream_key, dims, shards, -0.22, 0.18)
    return jnp.clip(values, -bound, bound).astype(held_as)


def setup_inputs(seed: int = 0) -> dict:
    arg_keys = jax.random.split(jax.random.key(seed), 14)
    queries = scatter_about(arg_keys[0], (TOKENS, HEADS * HD), 1.0, 6.0, ((0, 4), (1, 8)))
    key_heads = draw_key_heads(jax.random.fold_in(arg_keys[13], 71), 0)
    value_heads = draw_value_heads(jax.random.fold_in(arg_keys[13], 71), 0)
    out_gain = jnp.clip(1.0 + 0.18 * jax.random.normal(arg_keys[3], (HEADS * HD,), jnp.float32), 0.099609375, 1.8984375).astype(jnp.bfloat16)
    out_weight = scatter_about(arg_keys[4], (HEADS * HD, D), (HEADS * HD) ** -0.5, 0.09375, ((0, 8),))
    residual = draw_residual(jax.random.fold_in(arg_keys[13], 71), 0)
    norm_gain = jnp.clip(1.0 + 0.18 * jax.random.normal(arg_keys[6], (D,), jnp.float32), 0.099609375, 1.8984375).astype(jnp.bfloat16)
    routes_keys = jax.random.split(jax.random.fold_in(arg_keys[7], 1), TOKENS // TOK_DEV)
    routes_turns = jax.random.permutation(jax.random.fold_in(arg_keys[7], 3), TOKENS // TOK_DEV)
    routes = jax.vmap(lambda own, number: assign_block(jax.random.fold_in(arg_keys[7], 2), own, number, TOK_DEV, EXPERTS, TOPK, CAP, 2))(routes_keys, routes_turns).reshape((TOKENS, TOPK))
    route_weights = jnp.clip(0.02 + 0.38 * jax.random.uniform(arg_keys[8], (TOKENS, TOPK), jnp.float32) ** level_of(arg_keys[8], (TOKENS, TOPK), ((0, 32),), -0.2, 0.2), 0.02, 0.4)
    cotangent = scatter_about(arg_keys[9], (TOKENS, D), 1.0, 6.0, ((0, 32),))
    w_gate = scatter_about(arg_keys[10], (EXPERTS, D, FF), D ** -0.5, 0.125, ((0, 32),))
    w_up = scatter_about(arg_keys[11], (EXPERTS, D, FF), D ** -0.5, 0.125, ((0, 32),))
    w_down = scatter_about(arg_keys[12], (EXPERTS, FF, D), FF ** -0.5, 0.21875, ((0, 32),))
    return {"queries": queries, "key_heads": key_heads, "value_heads": value_heads, "out_gain": out_gain, "out_weight": out_weight, "residual": residual, "norm_gain": norm_gain, "routes": routes, "route_weights": route_weights, "cotangent": cotangent, "w_gate": w_gate, "w_up": w_up, "w_down": w_down}


epsilon = 1e-06
highest = lax.Precision.HIGHEST

def round_half(values):
    return lax.optimization_barrier(values.astype(jnp.bfloat16)).astype(jnp.float32)

def feature_map(values):
    widened = values.astype(jnp.float32)
    return round_half(jnp.where(widened > 0, widened + 1.0, jnp.exp(jnp.minimum(widened, 0.0))))

def rms_norm(values, gain):
    widened = values.astype(jnp.float32)
    inverse = lax.rsqrt(lax.optimization_barrier(jnp.mean(widened * widened, axis=-1, keepdims=True)) + epsilon)
    return (widened * inverse * gain.astype(jnp.float32)).astype(jnp.bfloat16)

def attend_blocks(query_raw, key_feat, value_wide, state_sum, key_sum, block_size):
    length = query_raw.shape[0]
    heads_here = key_feat.shape[1]
    head_size = key_feat.shape[2]
    causal_mask = jnp.tril(jnp.ones((block_size, block_size), jnp.bool_))

    def into_blocks(array_in):
        return array_in.reshape(length // block_size, block_size, heads_here, head_size)

    def one_block(carry, inputs):
        running_state, running_keys = carry
        query_block, key_block, value_block = inputs
        query_block = feature_map(query_block)
        scores = jnp.einsum('bhi,chi->hbc', query_block, key_block, precision=highest)
        scores = jnp.where(causal_mask[None], scores, 0.0)
        numerator = jnp.einsum('hbc,chj->bhj', scores, value_block, precision=highest)
        numerator = numerator + jnp.einsum('bhi,hij->bhj', query_block, running_state, precision=highest)
        denominator = jnp.einsum('hbc->bh', scores) + jnp.einsum('bhi,hi->bh', query_block, running_keys, precision=highest)
        result = (numerator / denominator[:, :, None]).astype(jnp.bfloat16)
        running_state = running_state + jnp.einsum('bhi,bhj->hij', key_block, value_block, precision=highest)
        running_keys = running_keys + lax.optimization_barrier(jnp.sum(key_block, axis=0))
        return ((running_state, running_keys), result)
    carry_out, outputs = lax.scan(one_block, (state_sum, key_sum), (into_blocks(query_raw), into_blocks(key_feat), into_blocks(value_wide)))
    return outputs.reshape(length, heads_here * head_size)

def expert_grads(rows_in, scaled, gate_mat, up_mat, down_mat):
    gate_pre = jnp.dot(rows_in, gate_mat, preferred_element_type=jnp.float32)
    up_pre = jnp.dot(rows_in, up_mat, preferred_element_type=jnp.float32)
    sigmoid_gate = jax.nn.sigmoid(gate_pre)
    active = gate_pre * sigmoid_gate
    hidden_units = (active * up_pre).astype(jnp.bfloat16)
    grad_down = lax.dot_general(hidden_units, scaled, (((0,), (0,)), ((), ())), preferred_element_type=jnp.float32).astype(jnp.bfloat16)
    grad_hidden = lax.dot_general(scaled, down_mat, (((1,), (1,)), ((), ())), preferred_element_type=jnp.float32)
    silu_slope = sigmoid_gate * (1.0 + gate_pre * (1.0 - sigmoid_gate))
    grad_pre_gate = (grad_hidden * up_pre * silu_slope).astype(jnp.bfloat16)
    grad_pre_up = (grad_hidden * active).astype(jnp.bfloat16)
    grad_gate = lax.dot_general(rows_in, grad_pre_gate, (((0,), (0,)), ((), ())), preferred_element_type=jnp.float32).astype(jnp.bfloat16)
    grad_up = lax.dot_general(rows_in, grad_pre_up, (((0,), (0,)), ((), ())), preferred_element_type=jnp.float32).astype(jnp.bfloat16)
    return (grad_gate, grad_up, grad_down)

def reference(queries, key_heads, value_heads, out_gain, out_weight, residual, norm_gain, routes, route_weights, cotangent, w_gate, w_up, w_down):
    block_size = min(512, TOKENS // N_CTX)
    key_feat = feature_map(key_heads.reshape(TOKENS, HEADS, HD))
    value_wide = value_heads.reshape(TOKENS, HEADS, HD).astype(jnp.float32)
    attention = attend_blocks(queries.reshape(TOKENS, HEADS, HD), key_feat, value_wide, jnp.zeros((HEADS, HD, HD), jnp.float32), jnp.zeros((HEADS, HD), jnp.float32), block_size)
    att_wide = attention.astype(jnp.float32)
    inv_rms = lax.rsqrt(lax.optimization_barrier(jnp.sum(att_wide * att_wide, axis=1)) / (HEADS * HD) + epsilon)
    normed = (att_wide * inv_rms[:, None] * out_gain.astype(jnp.float32)).astype(jnp.bfloat16)
    group_width = HEADS * HD // N_HEAD

    def add_group(group_index, running):
        start = (group_index * group_width).astype(jnp.int32)
        columns = lax.dynamic_slice_in_dim(normed, start, group_width, 1)
        weight_rows = lax.dynamic_slice_in_dim(out_weight, start, group_width, 0)
        return running + round_half(jnp.dot(columns, weight_rows, preferred_element_type=jnp.float32))
    projected = lax.fori_loop(0, N_HEAD, add_group, jnp.zeros((TOKENS, D), jnp.float32))
    hidden_out = (residual.astype(jnp.float32) + projected).astype(jnp.bfloat16)
    moe_in = rms_norm(hidden_out, norm_gain)
    blocks = TOKENS // TOK_DEV
    per_block = TOK_DEV * TOPK
    total_assign = blocks * per_block
    flat_routes = routes.reshape(blocks, per_block).astype(jnp.int32)
    onehot = (flat_routes[:, :, None] == jnp.arange(EXPERTS, dtype=jnp.int32)[None, None, :]).astype(jnp.int32)
    rank_in_block = lax.optimization_barrier(jnp.sum(jnp.cumsum(onehot, axis=1) * onehot, axis=2)) - 1
    position = jnp.arange(blocks, dtype=jnp.int32)[:, None] * CAP + rank_in_block
    slot_table = jnp.full((EXPERTS, blocks * CAP), total_assign, jnp.int32)
    slot_table = slot_table.at[flat_routes, position].set(jnp.arange(total_assign, dtype=jnp.int32).reshape(blocks, per_block))
    flat_weights = route_weights.reshape(total_assign)

    def per_expert(inputs):
        slot_list, gate_mat, up_mat, down_mat = inputs
        is_filled = slot_list < total_assign
        safe_index = jnp.minimum(slot_list, total_assign - 1)
        token_index = safe_index // TOPK
        rows_in = jnp.where(is_filled[:, None], moe_in[token_index], jnp.zeros((), jnp.bfloat16)).astype(jnp.bfloat16)
        weighted = flat_weights[safe_index][:, None] * cotangent[token_index].astype(jnp.float32)
        scaled = jnp.where(is_filled[:, None], weighted, 0.0).astype(jnp.bfloat16)
        return expert_grads(rows_in, scaled, gate_mat, up_mat, down_mat)
    grad_gate, grad_up, grad_down = lax.map(per_expert, (slot_table, w_gate, w_up, w_down))
    return (hidden_out, grad_gate, grad_up, grad_down)
```

```python
import functools

import jax
import jax.numpy as jnp
from jax import lax
from jax.experimental import pallas as pl
from jax.experimental.pallas import tpu as pltpu
from jax.sharding import PartitionSpec as P

HD = 128
EXPERTS = 128
TOPK = 8
SPAN = 8
MESH = pl.DeviceIdType.MESH
MIB = 1 << 20
epsilon = 1e-06
f32 = jnp.float32
bf16 = jnp.bfloat16


def feature_map(values):
    widened = values.astype(f32)
    return jnp.where(widened > 0, widened + 1.0, jnp.exp(jnp.minimum(widened, 0.0))).astype(bf16)


def rms_norm(values, gain):
    widened = values.astype(f32)
    inverse = lax.rsqrt(jnp.mean(widened * widened, axis=-1, keepdims=True) + epsilon)
    return (widened * inverse * gain.astype(f32)).astype(bf16)


def dot_tn(a, b):
    return lax.dot_general(a, b, (((0,), (0,)), ((), ())), preferred_element_type=f32)


def dot_nt(a, b):
    return lax.dot_general(a, b, (((1,), (1,)), ((), ())), preferred_element_type=f32)


def span_kernel(key_ref, value_ref, out_ref):
    feat = feature_map(key_ref[...])
    out_ref[0, :HD, :] = dot_tn(feat, value_ref[...]).astype(bf16)
    keys = jnp.sum(feat.astype(f32), axis=0, keepdims=True)
    row = lax.broadcasted_iota(jnp.int32, (16, HD), 0)
    out_ref[0, HD:, :] = jnp.where(row == 0, keys, 0.0).astype(bf16)


def span_sums(key_heads, value_heads):
    length, width = key_heads.shape
    heads = width // HD
    return pl.pallas_call(
        span_kernel,
        grid=(heads,),
        out_shape=jax.ShapeDtypeStruct((heads, HD + 16, HD), bf16),
        in_specs=[pl.BlockSpec((length, HD), lambda h: (0, h))] * 2,
        out_specs=pl.BlockSpec((1, HD + 16, HD), lambda h: (h, 0, 0)),
        compiler_params=pltpu.CompilerParams(vmem_limit_bytes=48 * MIB),
        name="span_sums",
    )(key_heads, value_heads)


def attend_kernel(block, place_ref, query_ref, key_ref, value_ref, sums_ref, gain_ref, out_ref, square_ref):
    head = pl.program_id(0)
    length = query_ref.shape[0]
    place = place_ref[0]
    state = jnp.zeros((HD, HD), f32)
    keys = jnp.zeros((1, HD), f32)
    for i in range(sums_ref.shape[0]):
        part = sums_ref[i, 0].astype(f32)
        state = state + jnp.where(i < place, part[:HD], 0.0)
        keys = keys + jnp.where(i < place, part[HD : HD + 1], 0.0)
    gain = gain_ref[...].astype(f32)
    row = lax.broadcasted_iota(jnp.int32, (block, block), 0)
    column = lax.broadcasted_iota(jnp.int32, (block, block), 1)
    for i in range(length // block):
        at = pl.ds(i * block, block)
        query = feature_map(query_ref[at, :])
        key = feature_map(key_ref[at, :])
        value = value_ref[at, :]
        scores = jnp.where(row >= column, dot_nt(query, key), 0.0)
        high = state.astype(bf16)
        low = (state - high.astype(f32)).astype(bf16)
        numerator = jnp.dot(scores.astype(bf16), value, preferred_element_type=f32)
        numerator = numerator + jnp.dot(query, high, preferred_element_type=f32)
        numerator = numerator + jnp.dot(query, low, preferred_element_type=f32)
        denominator = jnp.sum(scores, axis=1, keepdims=True)
        denominator = denominator + jnp.sum(query.astype(f32) * keys, axis=1, keepdims=True)
        result = (numerator / denominator).astype(bf16).astype(f32)
        out_ref[at, :] = (result * gain).astype(bf16)
        squares = result * result

        @pl.when(head == 0)
        def _():
            square_ref[at, :] = squares

        @pl.when(head != 0)
        def _():
            square_ref[at, :] = square_ref[at, :] + squares

        state = state + dot_tn(key, value)
        keys = keys + jnp.sum(key.astype(f32), axis=0, keepdims=True)


def attend(place, queries, key_heads, value_heads, sums, gain):
    length, width = queries.shape
    heads = width // HD
    block = 256 if length % 256 == 0 else length
    column = pl.BlockSpec((length, HD), lambda h: (0, h))
    return pl.pallas_call(
        functools.partial(attend_kernel, block),
        grid=(heads,),
        out_shape=[
            jax.ShapeDtypeStruct((length, width), bf16),
            jax.ShapeDtypeStruct((length, HD), f32),
        ],
        in_specs=[
            pl.BlockSpec(memory_space=pltpu.SMEM),
            column,
            column,
            column,
            pl.BlockSpec((sums.shape[0], 1, HD + 16, HD), lambda h: (0, h, 0, 0)),
            pl.BlockSpec((1, HD), lambda h: (0, h)),
        ],
        out_specs=[column, pl.BlockSpec((length, HD), lambda h: (0, 0))],
        compiler_params=pltpu.CompilerParams(vmem_limit_bytes=48 * MIB),
        name="attend",
    )(place, queries, key_heads, value_heads, sums, gain.reshape(1, width))


def gather_kernel(x_ref, out_ref, local_sem, zs, zr, ps, pr, ds, dr, ss, sr):
    rows = x_ref.shape[0]
    half = rows // 2
    i, h = lax.axis_index("ctx"), lax.axis_index("head")
    n_head = lax.axis_size("head")
    chips = n_head // 2
    k, c = h // 2, h % 2
    beside = (i // 2) * 2 + (1 - i % 2)
    above = (1 - i // 2) * 2 + i % 2
    across = 3 - i
    to_beside, to_above = (beside, h), (above, h)
    sibling = (i, k * 2 + 1 - c)
    right, left = (i, h + 2), (i, h - 2)

    barrier = pltpu.get_barrier_semaphore()
    for peer in (to_beside, to_above, sibling):
        pl.semaphore_signal(barrier, inc=1, device_id=peer, device_id_type=MESH)

    @pl.when(k > 0)
    def _():
        pl.semaphore_signal(barrier, inc=1, device_id=left, device_id_type=MESH)

    @pl.when(k < chips - 1)
    def _():
        pl.semaphore_signal(barrier, inc=1, device_id=right, device_id_type=MESH)

    peers = 3 + (k + chips - 1) // chips + (2 * chips - 2 - k) // chips
    pl.semaphore_wait(barrier, peers)

    def span(ctx, chip, part=None):
        start = ((ctx * n_head) + chip * 2 + c) * rows
        if part is None:
            return pl.ds(pl.multiple_of(start, 16), rows)
        return pl.ds(pl.multiple_of(start + part * half, 16), half)

    def send(src, at, send_sem, recv_sem, peer):
        return pltpu.make_async_remote_copy(
            src_ref=src, dst_ref=out_ref.at[at], send_sem=send_sem, recv_sem=recv_sem,
            device_id=peer, device_id_type=MESH,
        )

    def here(at):
        return out_ref.at[at]

    groups = 1 + 2 * (chips - 1)

    def chip_of(g):
        if g == 0:
            return k
        return k - 1 - (g - 1) // 2 if g % 2 == 1 else k + 1 + (g - 2) // 2

    def valid(g):
        if g == 0:
            return None
        return chip_of(g) >= 0 if g % 2 == 1 else chip_of(g) < chips

    def when(g, body):
        if valid(g) is None:
            body()
        else:
            pl.when(valid(g))(body)

    def plane(g):
        at = span(i, chip_of(g))
        src = x_ref if g == 0 else here(at)
        return [
            send(src, at, ps.at[g, 0], pr.at[g, 0], to_beside),
            send(src, at, ps.at[g, 1], pr.at[g, 1], to_above),
            send(src, at, ss.at[g, 0], sr.at[g, 0], sibling),
        ]

    def diagonal(g):
        chip = chip_of(g)
        top, bottom = span(beside, chip, 0), span(above, chip, 1)
        whole_b, whole_a = span(beside, chip), span(above, chip)
        return [
            send(here(top), top, ds.at[g, 0], dr.at[g, 0], to_above),
            send(here(bottom), bottom, ds.at[g, 1], dr.at[g, 1], to_beside),
            send(here(whole_b), whole_b, ss.at[g, 1], sr.at[g, 1], sibling),
            send(here(whole_a), whole_a, ss.at[g, 2], sr.at[g, 2], sibling),
        ]

    def last(g):
        at = span(across, chip_of(g))
        return [send(here(at), at, ss.at[g, 3], sr.at[g, 3], sibling)]

    def onward(g):
        at = span(i, chip_of(g))
        src = x_ref if g == 0 else here(at)
        copies = []
        if g == 0:
            copies.append((k < chips - 1, send(src, at, zs.at[1], zr.at[1], right)))
            copies.append((k > 0, send(src, at, zs.at[2], zr.at[2], left)))
        elif g + 2 < groups:
            go = k < chips - 1 if g % 2 == 1 else k > 0
            copies.append((go, send(src, at, zs.at[g + 2], zr.at[g + 2], right if g % 2 == 1 else left)))
        return copies

    def begin(g):
        def body():
            if g > 0:
                at = span(i, chip_of(g))
                send(here(at), at, zs.at[g], zr.at[g], left if g % 2 == 1 else right).wait_recv()
            for go, copy in onward(g):
                pl.when(go)(copy.start)
            for copy in plane(g):
                copy.start()

        when(g, body)

    def middle(g):
        def body():
            chip = chip_of(g)
            at = span(beside, chip)
            send(here(at), at, ps.at[g, 0], pr.at[g, 0], to_beside).wait_recv()
            at = span(above, chip)
            send(here(at), at, ps.at[g, 1], pr.at[g, 1], to_above).wait_recv()
            for copy in diagonal(g):
                copy.start()

        when(g, body)

    def finish(g):
        def body():
            chip = chip_of(g)
            at = span(across, chip, 0)
            send(here(at), at, ds.at[g, 0], dr.at[g, 0], to_above).wait_recv()
            at = span(across, chip, 1)
            send(here(at), at, ds.at[g, 1], dr.at[g, 1], to_beside).wait_recv()
            for copy in last(g):
                copy.start()

        when(g, body)

    def drain(g):
        def body():
            for copy in plane(g) + diagonal(g) + last(g):
                copy.wait_send()
            for go, copy in onward(g):
                pl.when(go)(copy.wait_send)
            chip = chip_of(g)
            for j, ctx in enumerate((i, beside, above, across)):
                start = ((ctx * n_head) + chip * 2 + 1 - c) * rows
                at = pl.ds(pl.multiple_of(start, 16), rows)
                send(here(at), at, ss.at[g, j], sr.at[g, j], sibling).wait_recv()

        when(g, body)

    own = pltpu.make_async_copy(x_ref, here(span(i, k)), local_sem)
    own.start()
    stages = [[0]] + [[1 + 2 * s, 2 + 2 * s] for s in range(chips - 1)]
    for s in range(len(stages) + 2):
        for step, late in ((begin, 0), (middle, 1), (finish, 2)):
            if 0 <= s - late < len(stages):
                for g in stages[s - late]:
                    step(g)
    own.wait()
    for g in range(groups):
        drain(g)


def gather_rows(x, devices, chips):
    groups = 1 + 2 * (chips - 1)
    dma = pltpu.SemaphoreType.DMA
    return pl.pallas_call(
        gather_kernel,
        out_shape=jax.ShapeDtypeStruct((devices * x.shape[0], x.shape[1]), x.dtype),
        in_specs=[pl.BlockSpec(memory_space=pl.ANY)],
        out_specs=pl.BlockSpec(memory_space=pl.ANY),
        scratch_shapes=[
            dma, dma((groups,)), dma((groups,)), dma((groups, 2)), dma((groups, 2)),
            dma((groups, 2)), dma((groups, 2)), dma((groups, 4)), dma((groups, 4)),
        ],
        compiler_params=pltpu.CompilerParams(collective_id=0, has_side_effects=True),
        name="gather_rows",
    )(x)


def pick_kernel(scale, target_ref, weight_ref, x_ref, out_ref):
    experts, slots = out_ref.shape[0], out_ref.shape[1]
    tokens = x_ref.shape[0]
    slot = lax.broadcasted_iota(jnp.int32, (slots, tokens), 0)
    for e in range(experts):
        chosen = slot == target_ref[e : e + 1, :]
        rows = jnp.dot(chosen.astype(f32).astype(bf16), x_ref[...], preferred_element_type=f32)
        if scale:
            weights = jnp.sum(jnp.where(chosen, weight_ref[e : e + 1, :], 0.0), axis=1, keepdims=True)
            rows = rows * weights
        out_ref[e] = rows.astype(bf16)


def pick(target, weight, x, capacity, block_rows, scale):
    experts, tokens = target.shape
    span = SPAN * block_rows
    slots = SPAN * capacity
    steps = tokens // span
    meta = pl.BlockSpec((experts, span), lambda s: (0, s))
    return pl.pallas_call(
        functools.partial(pick_kernel, scale),
        grid=(steps,),
        out_shape=jax.ShapeDtypeStruct((experts, steps * slots, x.shape[1]), bf16),
        in_specs=[meta, meta, pl.BlockSpec((span, x.shape[1]), lambda s: (s, 0))],
        out_specs=pl.BlockSpec((experts, slots, x.shape[1]), lambda s: (0, s, 0)),
        compiler_params=pltpu.CompilerParams(vmem_limit_bytes=56 * MIB),
        cost_estimate=pl.CostEstimate(
            flops=2 * experts * slots * tokens * x.shape[1],
            bytes_accessed=2 * x.size + 2 * experts * steps * slots * x.shape[1],
            transcendentals=0,
        ),
        name="pick_scaled" if scale else "pick_rows",
    )(target, weight, x)


def expert_kernel(rows_ref, scaled_ref, gate_ref, up_ref, down_ref, dgate_ref, dup_ref, ddown_ref, turned):
    @pl.when(pl.program_id(1) == 0)
    def _():
        turned[...] = rows_ref[0].T

    rows, scaled = rows_ref[0], scaled_ref[0]
    gate_pre = jnp.dot(rows, gate_ref[0], preferred_element_type=f32)
    up_pre = jnp.dot(rows, up_ref[0], preferred_element_type=f32)
    grad_hidden = dot_nt(scaled, down_ref[0])
    sigmoid_gate = jax.nn.sigmoid(gate_pre)
    active = gate_pre * sigmoid_gate
    hidden_units = (active * up_pre).astype(bf16)
    silu_slope = sigmoid_gate * (1.0 + gate_pre * (1.0 - sigmoid_gate))
    grad_pre_gate = (grad_hidden * up_pre * silu_slope).astype(bf16)
    grad_pre_up = (grad_hidden * active).astype(bf16)
    ddown_ref[0] = dot_tn(hidden_units, scaled).astype(bf16)
    dgate_ref[0] = jnp.dot(turned[...], grad_pre_gate, preferred_element_type=f32).astype(bf16)
    dup_ref[0] = jnp.dot(turned[...], grad_pre_up, preferred_element_type=f32).astype(bf16)


def expert_grads(rows_in, scaled, w_gate, w_up, w_down):
    experts, width, units = w_gate.shape
    slots = rows_in.shape[1]
    tile = 256 if units % 256 == 0 else units
    token = pl.BlockSpec((1, slots, width), lambda e, f: (e, 0, 0))
    wide = pl.BlockSpec((1, width, tile), lambda e, f: (e, 0, f))
    tall = pl.BlockSpec((1, tile, width), lambda e, f: (e, f, 0))
    return pl.pallas_call(
        expert_kernel,
        grid=(experts, units // tile),
        out_shape=[
            jax.ShapeDtypeStruct(w_gate.shape, bf16),
            jax.ShapeDtypeStruct(w_up.shape, bf16),
            jax.ShapeDtypeStruct(w_down.shape, bf16),
        ],
        in_specs=[token, token, wide, wide, tall],
        out_specs=[wide, wide, tall],
        scratch_shapes=[pltpu.VMEM((width, slots), bf16)],
        compiler_params=pltpu.CompilerParams(vmem_limit_bytes=58 * MIB),
        cost_estimate=pl.CostEstimate(
            flops=12 * experts * slots * width * units,
            bytes_accessed=12 * experts * width * units + 4 * experts * slots * width,
            transcendentals=experts * slots * units,
        ),
        name="expert_grads",
    )(rows_in, scaled, w_gate, w_up, w_down)


def exchange_slots(moe_in, routes, route_weights, cotangent, local_experts, capacity, devices):
    tok_here, width = moe_in.shape
    per_block = tok_here * TOPK
    flat = routes.reshape(per_block)
    onehot = (flat[:, None] == jnp.arange(EXPERTS, dtype=jnp.int32)[None, :]).astype(jnp.int32)
    rank = jnp.sum(jnp.cumsum(onehot, axis=0) * onehot, axis=1) - 1
    slot_rows = devices * capacity
    target = flat % local_experts * slot_rows + flat // local_experts * capacity + rank
    filler = jnp.full((local_experts * slot_rows,), per_block, jnp.int32)
    filler = filler.at[target].set(jnp.arange(per_block, dtype=jnp.int32))
    is_filled = (filler < per_block)[:, None]
    index = jnp.minimum(filler, per_block - 1)
    token = index // TOPK
    rows_in = jnp.where(is_filled, moe_in[token], jnp.zeros((), bf16))
    weighted = route_weights.reshape(per_block)[index][:, None] * cotangent[token].astype(f32)
    scaled = jnp.where(is_filled, weighted, 0.0).astype(bf16)
    return tuple(
        lax.all_to_all(
            a.reshape(local_experts, slot_rows, width), ("ctx", "head"), split_axis=1, concat_axis=1, tiled=True
        )
        for a in (rows_in, scaled)
    )


def on_device(
    queries, key_heads, value_heads, out_gain, out_weight, residual, norm_gain,
    routes, route_weights, cotangent, w_gate, w_up, w_down,
):
    both = ("ctx", "head")
    n_ctx, n_head = lax.axis_size("ctx"), lax.axis_size("head")
    devices = n_ctx * n_head
    tok_here, width = residual.shape
    local_experts = w_gate.shape[0]
    capacity = max(2, tok_here * TOPK * 5 // (EXPERTS * 4))
    whole = (
        n_ctx == 4 and n_head % 2 == 0 and devices % SPAN == 0
        and devices * tok_here <= 4 * local_experts * devices * capacity
    )

    if whole:
        with jax.named_scope("gather_cotangent"):
            cot_all = lax.all_gather(cotangent, both, axis=0, tiled=True)
            meta = jnp.concatenate([routes.astype(f32), route_weights], axis=1).T
            meta = lax.all_gather(meta, both, axis=0)

    sums = lax.all_gather(span_sums(key_heads, value_heads), "ctx")
    place = lax.axis_index("ctx").astype(jnp.int32).reshape(1)
    scaled_att, squares = attend(place, queries, key_heads, value_heads, sums, out_gain)
    partial = jnp.dot(scaled_att, out_weight, preferred_element_type=f32).astype(bf16)
    projected = lax.psum_scatter(partial, "head", scatter_dimension=0, tiled=True).astype(f32)
    total = lax.psum_scatter(jnp.sum(squares, axis=1), "head", scatter_dimension=0, tiled=True)
    inv_rms = lax.rsqrt(total / (queries.shape[1] * n_head) + epsilon)
    hidden_out = (residual.astype(f32) + projected * inv_rms[:, None]).astype(bf16)
    moe_in = rms_norm(hidden_out, norm_gain)

    if whole:
        with jax.named_scope("slots"):
            mine = (lax.axis_index(both) * local_experts).astype(f32) + jnp.arange(local_experts, dtype=f32)
            named = meta[None, :, :TOPK, :] == mine[:, None, None, None]
            weight = jnp.sum(jnp.where(named, meta[None, :, TOPK:, :], 0.0), axis=2)
            member = jnp.any(named, axis=2)
            before = jnp.triu(jnp.ones((tok_here, tok_here), bf16), 1)
            rank = jnp.dot(member.astype(bf16), before, preferred_element_type=f32).astype(jnp.int32)
            turn = (jnp.arange(devices, dtype=jnp.int32) % SPAN * capacity)[None, :, None]
            target = jnp.where(member, rank + turn, -1).reshape(local_experts, devices * tok_here)
            weight = weight.reshape(local_experts, devices * tok_here)
        scaled = pick(target, weight, cot_all, capacity, tok_here, True)
        rows_all = gather_rows(moe_in, devices, n_head // 2)
        rows_in = pick(target, weight, rows_all, capacity, tok_here, False)
    else:
        rows_in, scaled = exchange_slots(
            moe_in, routes, route_weights, cotangent, local_experts, capacity, devices
        )
    grad_gate, grad_up, grad_down = expert_grads(rows_in, scaled, w_gate, w_up, w_down)
    return (hidden_out, grad_gate, grad_up, grad_down)


def solution(mesh):
    tokens = P(("ctx", "head"), None)
    experts = P(("ctx", "head"), None, None)
    in_specs = (
        P("ctx", "head"), P("ctx", "head"), P("ctx", "head"), P("head"), P("head", None),
        tokens, P(), tokens, tokens, tokens, experts, experts, experts,
    )
    out_specs = (tokens, experts, experts, experts)
    return jax.shard_map(on_device, mesh=mesh, in_specs=in_specs, out_specs=out_specs, check_vma=False)
```

```python
import functools

import jax
import jax.numpy as jnp
from jax import lax
from jax.experimental import pallas as pl
from jax.experimental.pallas import tpu as pltpu
from jax.sharding import PartitionSpec as P

HD = 128
EXPERTS = 128
TOPK = 8
SPAN = 8
MESH = pl.DeviceIdType.MESH
MIB = 1 << 20
epsilon = 1e-06
f32 = jnp.float32
bf16 = jnp.bfloat16


def feature_map(values):
    widened = values.astype(f32)
    return jnp.where(widened > 0, widened + 1.0, jnp.exp(jnp.minimum(widened, 0.0))).astype(bf16)


def rms_norm(values, gain):
    widened = values.astype(f32)
    inverse = lax.rsqrt(jnp.mean(widened * widened, axis=-1, keepdims=True) + epsilon)
    return (widened * inverse * gain.astype(f32)).astype(bf16)


def dot_tn(a, b):
    return lax.dot_general(a, b, (((0,), (0,)), ((), ())), preferred_element_type=f32)


def dot_nt(a, b):
    return lax.dot_general(a, b, (((1,), (1,)), ((), ())), preferred_element_type=f32)


def span_kernel(key_ref, value_ref, out_ref):
    feat = feature_map(key_ref[...])
    out_ref[0, :HD, :] = dot_tn(feat, value_ref[...]).astype(bf16)
    keys = jnp.sum(feat.astype(f32), axis=0, keepdims=True)
    row = lax.broadcasted_iota(jnp.int32, (16, HD), 0)
    out_ref[0, HD:, :] = jnp.where(row == 0, keys, 0.0).astype(bf16)


def span_sums(key_heads, value_heads):
    length, width = key_heads.shape
    heads = width // HD
    return pl.pallas_call(
        span_kernel,
        grid=(heads,),
        out_shape=jax.ShapeDtypeStruct((heads, HD + 16, HD), bf16),
        in_specs=[pl.BlockSpec((length, HD), lambda h: (0, h))] * 2,
        out_specs=pl.BlockSpec((1, HD + 16, HD), lambda h: (h, 0, 0)),
        compiler_params=pltpu.CompilerParams(vmem_limit_bytes=48 * MIB),
        name="span_sums",
    )(key_heads, value_heads)


def attend_kernel(block, place_ref, query_ref, key_ref, value_ref, sums_ref, gain_ref, out_ref, square_ref):
    head = pl.program_id(0)
    length = query_ref.shape[0]
    place = place_ref[0]
    state = jnp.zeros((HD, HD), f32)
    keys = jnp.zeros((1, HD), f32)
    for i in range(sums_ref.shape[0]):
        part = sums_ref[i, 0].astype(f32)
        state = state + jnp.where(i < place, part[:HD], 0.0)
        keys = keys + jnp.where(i < place, part[HD : HD + 1], 0.0)
    gain = gain_ref[...].astype(f32)
    row = lax.broadcasted_iota(jnp.int32, (block, block), 0)
    column = lax.broadcasted_iota(jnp.int32, (block, block), 1)
    for i in range(length // block):
        at = pl.ds(i * block, block)
        query = feature_map(query_ref[at, :])
        key = feature_map(key_ref[at, :])
        value = value_ref[at, :]
        scores = jnp.where(row >= column, dot_nt(query, key), 0.0)
        high = state.astype(bf16)
        low = (state - high.astype(f32)).astype(bf16)
        numerator = jnp.dot(scores.astype(bf16), value, preferred_element_type=f32)
        numerator = numerator + jnp.dot(query, high, preferred_element_type=f32)
        numerator = numerator + jnp.dot(query, low, preferred_element_type=f32)
        denominator = jnp.sum(scores, axis=1, keepdims=True)
        denominator = denominator + jnp.sum(query.astype(f32) * keys, axis=1, keepdims=True)
        result = (numerator / denominator).astype(bf16).astype(f32)
        out_ref[at, :] = (result * gain).astype(bf16)
        squares = result * result

        @pl.when(head == 0)
        def _():
            square_ref[at, :] = squares

        @pl.when(head != 0)
        def _():
            square_ref[at, :] = square_ref[at, :] + squares

        state = state + dot_tn(key, value)
        keys = keys + jnp.sum(key.astype(f32), axis=0, keepdims=True)


def attend(place, queries, key_heads, value_heads, sums, gain):
    length, width = queries.shape
    heads = width // HD
    block = 256 if length % 256 == 0 else length
    column = pl.BlockSpec((length, HD), lambda h: (0, h))
    return pl.pallas_call(
        functools.partial(attend_kernel, block),
        grid=(heads,),
        out_shape=[
            jax.ShapeDtypeStruct((length, width), bf16),
            jax.ShapeDtypeStruct((length, HD), f32),
        ],
        in_specs=[
            pl.BlockSpec(memory_space=pltpu.SMEM),
            column,
            column,
            column,
            pl.BlockSpec((sums.shape[0], 1, HD + 16, HD), lambda h: (0, h, 0, 0)),
            pl.BlockSpec((1, HD), lambda h: (0, h)),
        ],
        out_specs=[column, pl.BlockSpec((length, HD), lambda h: (0, 0))],
        compiler_params=pltpu.CompilerParams(vmem_limit_bytes=48 * MIB),
        name="attend",
    )(place, queries, key_heads, value_heads, sums, gain.reshape(1, width))


def gather_kernel(x_ref, out_ref, local_sem, zs, zr, ps, pr, ds, dr, ss, sr, first=None, work=()):
    rows = x_ref.shape[0]
    half = rows // 2
    i, h = lax.axis_index("ctx"), lax.axis_index("head")
    n_head = lax.axis_size("head")
    chips = n_head // 2
    k, c = h // 2, h % 2
    beside = (i // 2) * 2 + (1 - i % 2)
    above = (1 - i // 2) * 2 + i % 2
    across = 3 - i
    to_beside, to_above = (beside, h), (above, h)
    sibling = (i, k * 2 + 1 - c)
    right, left = (i, h + 2), (i, h - 2)

    barrier = pltpu.get_barrier_semaphore()
    greeted = [to_beside, to_above, sibling] + ([(across, h)] if first else [])
    for peer in greeted:
        pl.semaphore_signal(barrier, inc=1, device_id=peer, device_id_type=MESH)

    @pl.when(k > 0)
    def _():
        pl.semaphore_signal(barrier, inc=1, device_id=left, device_id_type=MESH)

    @pl.when(k < chips - 1)
    def _():
        pl.semaphore_signal(barrier, inc=1, device_id=right, device_id_type=MESH)

    peers = len(greeted) + (k + chips - 1) // chips + (2 * chips - 2 - k) // chips
    pl.semaphore_wait(barrier, peers)

    def span(ctx, chip, part=None):
        start = ((ctx * n_head) + chip * 2 + c) * rows
        if part is None:
            return pl.ds(pl.multiple_of(start, 16), rows)
        return pl.ds(pl.multiple_of(start + part * half, 16), half)

    def send(src, at, send_sem, recv_sem, peer):
        return pltpu.make_async_remote_copy(
            src_ref=src, dst_ref=out_ref.at[at], send_sem=send_sem, recv_sem=recv_sem,
            device_id=peer, device_id_type=MESH,
        )

    def here(at):
        return out_ref.at[at]

    groups = 1 + 2 * (chips - 1)

    def chip_of(g):
        if g == 0:
            return k
        return k - 1 - (g - 1) // 2 if g % 2 == 1 else k + 1 + (g - 2) // 2

    def valid(g):
        if g == 0:
            return None
        return chip_of(g) >= 0 if g % 2 == 1 else chip_of(g) < chips

    def when(g, body):
        if valid(g) is None:
            body()
        else:
            pl.when(valid(g))(body)

    def plane(g):
        at = span(i, chip_of(g))
        src = x_ref if g == 0 else here(at)
        return [
            send(src, at, ps.at[g, 0], pr.at[g, 0], to_beside),
            send(src, at, ps.at[g, 1], pr.at[g, 1], to_above),
            send(src, at, ss.at[g, 0], sr.at[g, 0], sibling),
        ]

    def diagonal(g):
        chip = chip_of(g)
        top, bottom = span(beside, chip, 0), span(above, chip, 1)
        whole_b, whole_a = span(beside, chip), span(above, chip)
        return [
            send(here(top), top, ds.at[g, 0], dr.at[g, 0], to_above),
            send(here(bottom), bottom, ds.at[g, 1], dr.at[g, 1], to_beside),
            send(here(whole_b), whole_b, ss.at[g, 1], sr.at[g, 1], sibling),
            send(here(whole_a), whole_a, ss.at[g, 2], sr.at[g, 2], sibling),
        ]

    def last(g):
        at = span(across, chip_of(g))
        return [send(here(at), at, ss.at[g, 3], sr.at[g, 3], sibling)]

    def onward(g):
        at = span(i, chip_of(g))
        src = x_ref if g == 0 else here(at)
        copies = []
        if g == 0:
            copies.append((k < chips - 1, send(src, at, zs.at[1], zr.at[1], right)))
            copies.append((k > 0, send(src, at, zs.at[2], zr.at[2], left)))
        elif g + 2 < groups:
            go = k < chips - 1 if g % 2 == 1 else k > 0
            copies.append((go, send(src, at, zs.at[g + 2], zr.at[g + 2], right if g % 2 == 1 else left)))
        return copies

    def begin(g):
        def body():
            if g > 0:
                at = span(i, chip_of(g))
                send(here(at), at, zs.at[g], zr.at[g], left if g % 2 == 1 else right).wait_recv()
            for go, copy in onward(g):
                pl.when(go)(copy.start)
            for copy in plane(g):
                copy.start()

        when(g, body)

    def middle(g):
        def body():
            chip = chip_of(g)
            at = span(beside, chip)
            send(here(at), at, ps.at[g, 0], pr.at[g, 0], to_beside).wait_recv()
            at = span(above, chip)
            send(here(at), at, ps.at[g, 1], pr.at[g, 1], to_above).wait_recv()
            for copy in diagonal(g):
                copy.start()

        when(g, body)

    def finish(g):
        def body():
            chip = chip_of(g)
            at = span(across, chip, 0)
            send(here(at), at, ds.at[g, 0], dr.at[g, 0], to_above).wait_recv()
            at = span(across, chip, 1)
            send(here(at), at, ds.at[g, 1], dr.at[g, 1], to_beside).wait_recv()
            for copy in last(g):
                copy.start()

        when(g, body)

    def drain(g):
        def body():
            for copy in plane(g) + diagonal(g) + last(g):
                copy.wait_send()
            for go, copy in onward(g):
                pl.when(go)(copy.wait_send)
            chip = chip_of(g)
            for j, ctx in enumerate((i, beside, above, across)):
                start = ((ctx * n_head) + chip * 2 + 1 - c) * rows
                at = pl.ds(pl.multiple_of(start, 16), rows)
                send(here(at), at, ss.at[g, j], sr.at[g, j], sibling).wait_recv()

        when(g, body)

    if first:
        first(i, (to_beside, to_above, (across, h)))
    own = pltpu.make_async_copy(x_ref, here(span(i, k)), local_sem)
    own.start()
    stages = [[0]] + [[1 + 2 * s, 2 + 2 * s] for s in range(chips - 1)]
    for s in range(len(stages) + 2):
        for step, late in ((begin, 0), (middle, 1), (finish, 2)):
            if 0 <= s - late < len(stages):
                for g in stages[s - late]:
                    step(g)
        if s < len(work):
            work[s](i)
    own.wait()
    for g in range(groups):
        drain(g)


def gather_sems(chips):
    groups = 1 + 2 * (chips - 1)
    dma = pltpu.SemaphoreType.DMA
    return [
        dma, dma((groups,)), dma((groups,)), dma((groups, 2)), dma((groups, 2)),
        dma((groups, 2)), dma((groups, 2)), dma((groups, 4)), dma((groups, 4)),
    ]


def gather_rows(x, devices, chips):
    return pl.pallas_call(
        gather_kernel,
        out_shape=jax.ShapeDtypeStruct((devices * x.shape[0], x.shape[1]), x.dtype),
        in_specs=[pl.BlockSpec(memory_space=pl.ANY)],
        out_specs=pl.BlockSpec(memory_space=pl.ANY),
        scratch_shapes=gather_sems(chips),
        compiler_params=pltpu.CompilerParams(collective_id=0, has_side_effects=True),
        name="gather_rows",
    )(x)


def front_kernel(
    block, x_ref, query_ref, key_ref, value_ref, gain_ref, weight_ref,
    out_ref, partial_ref, square_ref, own, sums, att, sum_send, sum_recv, *sems
):
    length, width = query_ref.shape
    heads = width // HD
    tall = 256 if length % 256 == 0 else length

    def columns(h):
        return pl.ds(pl.multiple_of(h * HD, HD), HD)

    def span_step(h, carry):
        feat = feature_map(key_ref[:, columns(h)])
        own[h, :HD, :] = dot_tn(feat, value_ref[:, columns(h)]).astype(bf16)
        keys = jnp.sum(feat.astype(f32), axis=0, keepdims=True)
        row = lax.broadcasted_iota(jnp.int32, (16, HD), 0)
        own[h, HD:, :] = jnp.where(row == 0, keys, 0.0).astype(bf16)
        return carry

    lax.fori_loop(0, heads, span_step, 0)
    square_ref[...] = jnp.zeros_like(square_ref)
    exchanged = []

    def first(i, peers):
        for j, peer in enumerate(peers):
            copy = pltpu.make_async_remote_copy(
                src_ref=own, dst_ref=sums.at[j], send_sem=sum_send.at[j], recv_sem=sum_recv.at[j],
                device_id=peer, device_id_type=MESH,
            )
            copy.start()
            exchanged.append(copy)

    def attention(i):
        for copy in exchanged:
            copy.wait()
        places = ((i // 2) * 2 + (1 - i % 2), (1 - i // 2) * 2 + i % 2, 3 - i)
        row = lax.broadcasted_iota(jnp.int32, (block, block), 0)
        column = lax.broadcasted_iota(jnp.int32, (block, block), 1)

        def head_step(h, carry):
            state = jnp.zeros((HD, HD), f32)
            keys = jnp.zeros((1, HD), f32)
            for j, place in enumerate(places):
                earlier = place < i
                state = state + jnp.where(earlier, sums[j, h, :HD, :].astype(f32), 0.0)
                keys = keys + jnp.where(earlier, sums[j, h, HD:, :].astype(f32)[:1], 0.0)
            gain = gain_ref[:, columns(h)].astype(f32)
            for n in range(length // block):
                at = pl.ds(n * block, block)
                query = feature_map(query_ref[at, columns(h)])
                key = feature_map(key_ref[at, columns(h)])
                value = value_ref[at, columns(h)]
                scores = jnp.where(row >= column, dot_nt(query, key), 0.0)
                high = state.astype(bf16)
                low = (state - high.astype(f32)).astype(bf16)
                numerator = jnp.dot(scores.astype(bf16), value, preferred_element_type=f32)
                numerator = numerator + jnp.dot(query, high, preferred_element_type=f32)
                numerator = numerator + jnp.dot(query, low, preferred_element_type=f32)
                denominator = jnp.sum(scores, axis=1, keepdims=True)
                denominator = denominator + jnp.sum(query.astype(f32) * keys, axis=1, keepdims=True)
                result = (numerator / denominator).astype(bf16).astype(f32)
                att[at, columns(h)] = (result * gain).astype(bf16)
                square_ref[at, :] = square_ref[at, :] + result * result
                state = state + dot_tn(key, value)
                keys = keys + jnp.sum(key.astype(f32), axis=0, keepdims=True)
            return carry

        lax.fori_loop(0, heads, head_step, 0)

    def project(i):
        def step(n, carry):
            at = pl.ds(pl.multiple_of(n * tall, 16), tall)
            product = jnp.dot(att[at, :], weight_ref[...], preferred_element_type=f32)
            partial_ref[at, :] = product.astype(bf16)
            return carry

        lax.fori_loop(0, length // tall, step, 0)

    gather_kernel(x_ref, out_ref, *sems, first=first, work=(attention, project))


def front(cotangent, queries, key_heads, value_heads, gain, out_weight, devices, chips):
    length, width = queries.shape
    heads = width // HD
    block = 256 if length % 256 == 0 else length
    vmem = pl.BlockSpec(memory_space=pltpu.VMEM)
    hbm = pl.BlockSpec(memory_space=pl.ANY)
    dma = pltpu.SemaphoreType.DMA
    return pl.pallas_call(
        functools.partial(front_kernel, block),
        out_shape=[
            jax.ShapeDtypeStruct((devices * cotangent.shape[0], cotangent.shape[1]), bf16),
            jax.ShapeDtypeStruct((length, out_weight.shape[1]), bf16),
            jax.ShapeDtypeStruct((length, HD), f32),
        ],
        in_specs=[hbm, vmem, vmem, vmem, vmem, vmem],
        out_specs=[hbm, vmem, vmem],
        scratch_shapes=[
            pltpu.VMEM((heads, HD + 16, HD), bf16),
            pltpu.VMEM((3, heads, HD + 16, HD), bf16),
            pltpu.VMEM((length, width), bf16),
            dma((3,)),
            dma((3,)),
        ] + gather_sems(chips),
        compiler_params=pltpu.CompilerParams(
            collective_id=1, has_side_effects=True, vmem_limit_bytes=40 * MIB
        ),
        name="front",
    )(cotangent, queries, key_heads, value_heads, gain.reshape(1, width), out_weight)


def pick_kernel(scale, target_ref, weight_ref, x_ref, out_ref, chosen_ref):
    experts, slots = out_ref.shape[0], out_ref.shape[1]
    tokens = x_ref.shape[0]
    slot = lax.broadcasted_iota(jnp.int32, (slots, tokens), 0)
    weights = []
    for e in range(experts):
        chosen = slot == target_ref[e : e + 1, :]
        chosen_ref[e * slots : (e + 1) * slots, :] = chosen.astype(f32).astype(bf16)
        if scale:
            weights.append(jnp.sum(jnp.where(chosen, weight_ref[e : e + 1, :], 0.0), axis=1, keepdims=True))
    rows = jnp.dot(chosen_ref[...], x_ref[...], preferred_element_type=f32)
    for e in range(experts):
        part = rows[e * slots : (e + 1) * slots]
        out_ref[e] = (part * weights[e] if scale else part).astype(bf16)


def pick(target, weight, x, capacity, block_rows, scale):
    experts, tokens = target.shape
    span = SPAN * block_rows
    slots = SPAN * capacity
    steps = tokens // span
    meta = pl.BlockSpec((experts, span), lambda s: (0, s))
    return pl.pallas_call(
        functools.partial(pick_kernel, scale),
        grid=(steps,),
        out_shape=jax.ShapeDtypeStruct((experts, steps * slots, x.shape[1]), bf16),
        in_specs=[meta, meta, pl.BlockSpec((span, x.shape[1]), lambda s: (s, 0))],
        out_specs=pl.BlockSpec((experts, slots, x.shape[1]), lambda s: (0, s, 0)),
        scratch_shapes=[pltpu.VMEM((experts * slots, span), bf16)],
        compiler_params=pltpu.CompilerParams(vmem_limit_bytes=56 * MIB),
        cost_estimate=pl.CostEstimate(
            flops=2 * experts * slots * tokens * x.shape[1],
            bytes_accessed=2 * x.size + 2 * experts * steps * slots * x.shape[1],
            transcendentals=0,
        ),
        name="pick_scaled" if scale else "pick_rows",
    )(target, weight, x)


def expert_kernel(rows_ref, scaled_ref, gate_ref, up_ref, down_ref, dgate_ref, dup_ref, ddown_ref, turned):
    @pl.when(pl.program_id(1) == 0)
    def _():
        turned[...] = rows_ref[0].T

    rows, scaled = rows_ref[0], scaled_ref[0]
    gate_pre = jnp.dot(rows, gate_ref[0], preferred_element_type=f32)
    up_pre = jnp.dot(rows, up_ref[0], preferred_element_type=f32)
    grad_hidden = dot_nt(scaled, down_ref[0])
    sigmoid_gate = jax.nn.sigmoid(gate_pre)
    active = gate_pre * sigmoid_gate
    hidden_units = (active * up_pre).astype(bf16)
    silu_slope = sigmoid_gate * (1.0 + gate_pre * (1.0 - sigmoid_gate))
    grad_pre_gate = (grad_hidden * up_pre * silu_slope).astype(bf16)
    grad_pre_up = (grad_hidden * active).astype(bf16)
    ddown_ref[0] = dot_tn(hidden_units, scaled).astype(bf16)
    dgate_ref[0] = jnp.dot(turned[...], grad_pre_gate, preferred_element_type=f32).astype(bf16)
    dup_ref[0] = jnp.dot(turned[...], grad_pre_up, preferred_element_type=f32).astype(bf16)


def expert_grads(rows_in, scaled, w_gate, w_up, w_down):
    experts, width, units = w_gate.shape
    slots = rows_in.shape[1]
    tile = 256 if units % 256 == 0 else units
    token = pl.BlockSpec((1, slots, width), lambda e, f: (e, 0, 0))
    wide = pl.BlockSpec((1, width, tile), lambda e, f: (e, 0, f))
    tall = pl.BlockSpec((1, tile, width), lambda e, f: (e, f, 0))
    return pl.pallas_call(
        expert_kernel,
        grid=(experts, units // tile),
        out_shape=[
            jax.ShapeDtypeStruct(w_gate.shape, bf16),
            jax.ShapeDtypeStruct(w_up.shape, bf16),
            jax.ShapeDtypeStruct(w_down.shape, bf16),
        ],
        in_specs=[token, token, wide, wide, tall],
        out_specs=[wide, wide, tall],
        scratch_shapes=[pltpu.VMEM((width, slots), bf16)],
        compiler_params=pltpu.CompilerParams(vmem_limit_bytes=58 * MIB),
        cost_estimate=pl.CostEstimate(
            flops=12 * experts * slots * width * units,
            bytes_accessed=12 * experts * width * units + 4 * experts * slots * width,
            transcendentals=experts * slots * units,
        ),
        name="expert_grads",
    )(rows_in, scaled, w_gate, w_up, w_down)


def exchange_slots(moe_in, routes, route_weights, cotangent, local_experts, capacity, devices):
    tok_here, width = moe_in.shape
    per_block = tok_here * TOPK
    flat = routes.reshape(per_block)
    onehot = (flat[:, None] == jnp.arange(EXPERTS, dtype=jnp.int32)[None, :]).astype(jnp.int32)
    rank = jnp.sum(jnp.cumsum(onehot, axis=0) * onehot, axis=1) - 1
    slot_rows = devices * capacity
    target = flat % local_experts * slot_rows + flat // local_experts * capacity + rank
    filler = jnp.full((local_experts * slot_rows,), per_block, jnp.int32)
    filler = filler.at[target].set(jnp.arange(per_block, dtype=jnp.int32))
    is_filled = (filler < per_block)[:, None]
    index = jnp.minimum(filler, per_block - 1)
    token = index // TOPK
    rows_in = jnp.where(is_filled, moe_in[token], jnp.zeros((), bf16))
    weighted = route_weights.reshape(per_block)[index][:, None] * cotangent[token].astype(f32)
    scaled = jnp.where(is_filled, weighted, 0.0).astype(bf16)
    return tuple(
        lax.all_to_all(
            a.reshape(local_experts, slot_rows, width), ("ctx", "head"), split_axis=1, concat_axis=1, tiled=True
        )
        for a in (rows_in, scaled)
    )


def on_device(
    queries, key_heads, value_heads, out_gain, out_weight, residual, norm_gain,
    routes, route_weights, cotangent, w_gate, w_up, w_down,
):
    both = ("ctx", "head")
    n_ctx, n_head = lax.axis_size("ctx"), lax.axis_size("head")
    devices = n_ctx * n_head
    tok_here, width = residual.shape
    local_experts = w_gate.shape[0]
    capacity = max(2, tok_here * TOPK * 5 // (EXPERTS * 4))
    whole = (
        n_ctx == 4 and n_head % 2 == 0 and devices % SPAN == 0
        and devices * tok_here <= 4 * local_experts * devices * capacity
    )

    if whole:
        cot_all, partial, squares = front(
            cotangent, queries, key_heads, value_heads, out_gain, out_weight, devices, n_head // 2
        )
        meta = jnp.concatenate([routes.astype(f32), route_weights], axis=1).T
        meta, partial = lax.optimization_barrier((meta, partial))
        meta = lax.all_gather(meta, both, axis=0)
    else:
        sums = lax.all_gather(span_sums(key_heads, value_heads), "ctx")
        place = lax.axis_index("ctx").astype(jnp.int32).reshape(1)
        scaled_att, squares = attend(place, queries, key_heads, value_heads, sums, out_gain)
        partial = jnp.dot(scaled_att, out_weight, preferred_element_type=f32).astype(bf16)
    projected = lax.psum_scatter(partial, "head", scatter_dimension=0, tiled=True).astype(f32)
    total = lax.psum_scatter(jnp.sum(squares, axis=1), "head", scatter_dimension=0, tiled=True)
    inv_rms = lax.rsqrt(total / (queries.shape[1] * n_head) + epsilon)
    hidden_out = (residual.astype(f32) + projected * inv_rms[:, None]).astype(bf16)
    moe_in = rms_norm(hidden_out, norm_gain)

    if whole:
        with jax.named_scope("slots"):
            mine = (lax.axis_index(both) * local_experts).astype(f32) + jnp.arange(local_experts, dtype=f32)
            named = meta[None, :, :TOPK, :] == mine[:, None, None, None]
            weight = jnp.sum(jnp.where(named, meta[None, :, TOPK:, :], 0.0), axis=2)
            member = jnp.any(named, axis=2)
            before = jnp.triu(jnp.ones((tok_here, tok_here), bf16), 1)
            rank = jnp.dot(member.astype(bf16), before, preferred_element_type=f32).astype(jnp.int32)
            turn = (jnp.arange(devices, dtype=jnp.int32) % SPAN * capacity)[None, :, None]
            target = jnp.where(member, rank + turn, -1).reshape(local_experts, devices * tok_here)
            weight = weight.reshape(local_experts, devices * tok_here)
        scaled = pick(target, weight, cot_all, capacity, tok_here, True)
        rows_all = gather_rows(moe_in, devices, n_head // 2)
        rows_in = pick(target, weight, rows_all, capacity, tok_here, False)
    else:
        rows_in, scaled = exchange_slots(
            moe_in, routes, route_weights, cotangent, local_experts, capacity, devices
        )
    grad_gate, grad_up, grad_down = expert_grads(rows_in, scaled, w_gate, w_up, w_down)
    return (hidden_out, grad_gate, grad_up, grad_down)


def solution(mesh):
    tokens = P(("ctx", "head"), None)
    experts = P(("ctx", "head"), None, None)
    in_specs = (
        P("ctx", "head"), P("ctx", "head"), P("ctx", "head"), P("head"), P("head", None),
        tokens, P(), tokens, tokens, tokens, experts, experts, experts,
    )
    out_specs = (tokens, experts, experts, experts)
    return jax.shard_map(on_device, mesh=mesh, in_specs=in_specs, out_specs=out_specs, check_vma=False)
```
